256 devices in a mesh: frame: 8 (over x, y_hi), space: 8 (over z), mp: 4 (over y_lo, core).
Axes of the slice: x: 4, y: 4 (y_hi: 2, y_lo: 2; y = y_hi * 2 + y_lo), z: 8, core: 2. Of those that a mesh axis runs over, the one named last changes fastest.
Arguments:
- latents: bfloat16 [8, 768, 5120], P('frame', 'space', 'mp'), may hold values from -40 to 40
- levels: int32 [8], P('frame'), may hold values from 0 to 49, as said below
- window_mask: int32 [8, 3, 768], P('frame'), may hold values from 0 to 1, as said below
- level_table: float32 [50, 3, 5120], replicated, may hold values from -4 to 4
- w_qkv: bfloat16 [5120, 32, 384], P(None, ('space', 'mp')), may hold values from -0.078125 to 0.078125
- gain_q: float32 [32, 128], P(('space', 'mp')), may hold values from 0.6 to 1.9
- gain_k: float32 [32, 128], P(('space', 'mp')), may hold values from 0.6 to 1.9
- w_out: bfloat16 [32, 128, 5120], P(('space', 'mp')), may hold values from -0.09375 to 0.09375
Outputs:
- hidden_state: bfloat16 [8, 768, 5120], P('frame', 'space', 'mp')
The draws below stay inside these ranges and needn't reach their ends.
Inputs may be any that keep to these rules, and one draw needn't show every extreme that they name: The frames' levels are distinct. window_mask[f, 0, k] is 1 for every frame f and token k.
All inputs are finite; a program needn't handle non-finite values.
Results may differ from the reference program's by a relative error of at most 0.012.
Values may be sent and summed in bfloat16 or wider, within the bound.
No kernel may reach another device: no remote copies, remote signals or barrier semaphores. Data moves between devices by JAX's collectives and lax.ppermute only.
A program may use at most 128 MiB of HBM per device.

```python
import math
import jax
import jax.numpy as jnp
from jax import lax

D = 5120
HD = 128
WINDOW = 3
LEVELS = 50
HEADS = 32
TOKENS = 768
FRAMES = 8


def ramp_scales(key, low, high):
    position = jnp.arange(D, dtype=jnp.float32) / (D - 1)
    rough = jnp.exp(jax.random.uniform(key, (D,), jnp.float32, -0.4, 0.4))
    ramp = jnp.exp(math.log(low) + (math.log(high) - math.log(low)) * position)
    return (ramp * rough)[None, None, :]


def draw_latents(key, part):
    key = jax.random.fold_in(key, 11)
    key_rows, key_cols, key_base = jax.random.split(key, 3)
    row_scale = jnp.exp(jax.random.uniform(key_rows, (FRAMES, TOKENS, 1), jnp.float32, math.log(0.3), math.log(3.0)))
    col_scale = ramp_scales(key_cols, 0.3, 3.0)
    base = jnp.clip(jax.random.normal(key_base, (FRAMES, TOKENS, D), jnp.float32), -4.0, 4.0)
    return jnp.clip(base * row_scale * col_scale, -40.0, 40.0).astype(jnp.bfloat16)


def draw_levels(key, part):
    key = jax.random.fold_in(key, 7)
    key_start, key_stride = jax.random.split(key, 2)
    rotation = jax.random.randint(key_start, (), 0, FRAMES)
    stride = jax.random.randint(key_stride, (), 1, LEVELS // FRAMES + 1)
    frame_index = jnp.arange(FRAMES, dtype=jnp.int32)
    return (LEVELS - 1 - (frame_index + rotation) % FRAMES * stride).astype(jnp.int32)


def draw_window_mask(key, part):
    key = jax.random.fold_in(key, 5)
    random_bits = (jax.random.randint(key, (FRAMES, WINDOW, TOKENS), 0, 4) != 0).astype(jnp.int32)
    back_index = jnp.arange(WINDOW, dtype=jnp.int32)[None, :, None]
    random_bits = jnp.where(back_index == 0, 1, random_bits)
    return random_bits.astype(jnp.int32)


def steps_of(rng, shape, pieces, smallest, high):
    def one(dim, blocks):
        draws = jax.random.uniform(jax.random.fold_in(jax.random.fold_in(rng, 6), dim), (blocks,), jnp.float32, smallest / len(pieces), high / len(pieces))
        return jnp.repeat(jnp.exp(draws), shape[dim] // blocks).reshape((-1,) + (1,) * (len(shape) - dim - 1))

    loudness = one(*pieces[0])
    for cut in pieces[1:]:
        loudness = loudness * one(*cut)
    return loudness


def noise(stream_key, dims, scale, most, shards=(), held_as=jnp.bfloat16):
    entries = scale * jax.random.normal(stream_key, dims, jnp.float32)
    if shards:
        entries = entries * steps_of(stream_key, dims, shards, -0.22, 0.18)
    return jnp.clip(entries, -most, most).astype(held_as)


def setup_inputs(seed: int = 0) -> dict:
    key_of = jax.random.split(jax.random.key(seed), 9)
    latents = draw_latents(jax.random.fold_in(key_of[8], 71), 0)
    levels = draw_levels(jax.random.fold_in(key_of[8], 71), 0)
    window_mask = draw_window_mask(jax.random.fold_in(key_of[8], 71), 0)
    level_table = noise(key_of[3], (LEVELS, 3, D), 1.0, 4.0, (), jnp.float32)
    w_qkv = noise(key_of[4], (D, HEADS, 3 * HD), D ** -0.5, 0.078125, ((1, 32),))
    gain_q = jnp.clip(jnp.exp(math.log(1.9) - 1.1526795 * jax.random.uniform(key_of[5], (HEADS, HD), jnp.float32) ** steps_of(key_of[5], (HEADS, HD), ((0, 32),), -0.2, 0.2)), 0.6, 1.9)
    gain_k = jnp.clip(jnp.exp(math.log(1.9) - 1.1526795 * jax.random.uniform(key_of[6], (HEADS, HD), jnp.float32) ** steps_of(key_of[6], (HEADS, HD), ((0, 32),), -0.2, 0.2)), 0.6, 1.9)
    w_out = noise(key_of[7], (HEADS, HD, D), (HEADS * HD) ** -0.5, 0.09375, ((0, 32),))
    return dict(latents=latents, levels=levels, window_mask=window_mask, level_table=level_table, w_qkv=w_qkv, gain_q=gain_q, gain_k=gain_k, w_out=w_out)


EPS = 1e-06

def reference(latents, levels, window_mask, level_table, w_qkv, gain_q, gain_k, w_out):
    features = latents.astype(jnp.float32)
    frames, tokens, model_width = features.shape
    head_size = gain_q.shape[1]
    modulation = level_table[levels]
    shift_part = modulation[:, 0][:, None, :]
    scale_part = modulation[:, 1][:, None, :]
    gate_part = modulation[:, 2][:, None, :]
    average = lax.optimization_barrier(jnp.sum(features, -1, keepdims=True)) / model_width
    spread = lax.optimization_barrier(jnp.sum(features * features, -1, keepdims=True)) / model_width - average * average
    normed = ((features - average) * lax.rsqrt(spread + EPS) * (1.0 + scale_part) + shift_part).astype(jnp.bfloat16)
    flat_rows = normed.reshape(frames * tokens, model_width)
    allowed = window_mask.astype(jnp.float32)

    def per_head(summed, head_index):
        weights = lax.dynamic_index_in_dim(w_qkv, head_index, 1, keepdims=False)
        mixed = jnp.dot(flat_rows, weights, preferred_element_type=jnp.float32).reshape(frames, tokens, 3 * head_size)
        query = mixed[..., :head_size]
        keyed = mixed[..., head_size:2 * head_size]
        valued = mixed[..., 2 * head_size:].astype(jnp.bfloat16)
        query_gain = lax.dynamic_index_in_dim(gain_q, head_index, 0, keepdims=False)
        key_gain = lax.dynamic_index_in_dim(gain_k, head_index, 0, keepdims=False)
        query = (query * lax.rsqrt(lax.optimization_barrier(jnp.mean(query * query, -1, keepdims=True)) + EPS) * query_gain).astype(jnp.bfloat16)
        keyed = (keyed * lax.rsqrt(lax.optimization_barrier(jnp.mean(keyed * keyed, -1, keepdims=True)) + EPS) * key_gain).astype(jnp.bfloat16)
        context_keys = jnp.stack([jnp.roll(keyed, back_step, axis=0) for back_step in range(3)], axis=1)
        context_values = jnp.stack([jnp.roll(valued, back_step, axis=0) for back_step in range(3)], axis=1)
        scores = jnp.einsum('ftc,fdkc->ftdk', query.astype(jnp.float32), context_keys.astype(jnp.float32)) / math.sqrt(head_size)
        expo = jnp.exp(scores) * allowed[:, None, :, :]
        probs = (expo / lax.optimization_barrier(jnp.sum(expo, axis=(2, 3), keepdims=True))).astype(jnp.bfloat16)
        attended = jnp.einsum('ftdk,fdkc->ftc', probs.astype(jnp.float32), context_values.astype(jnp.float32)).astype(jnp.bfloat16)
        out_weight = lax.dynamic_index_in_dim(w_out, head_index, 0, keepdims=False)
        head_term = jnp.dot(attended.reshape(frames * tokens, head_size), out_weight, preferred_element_type=jnp.float32).astype(jnp.bfloat16)
        head_term = lax.optimization_barrier(head_term).astype(jnp.float32)
        return (summed + head_term, None)
    start_sum = jnp.zeros((frames * tokens, model_width), jnp.float32)
    summed, _ = lax.scan(per_head, start_sum, jnp.arange(w_qkv.shape[1], dtype=jnp.int32))
    attn_sum = summed.reshape(frames, tokens, model_width)
    return (features + gate_part * attn_sum).astype(jnp.bfloat16)
```

```python
import math

import jax
import jax.numpy as jnp
from jax import lax
from jax.sharding import PartitionSpec as P

EPS = 1e-06
BF16 = jnp.bfloat16
F32 = jnp.float32


def shifted(value, axis, steps):
    count = lax.axis_size(axis)
    pairs = [(source, (source + steps) % count) for source in range(count)]
    return lax.ppermute(value, axis, pairs)


def swapped(value, flip):
    return lax.ppermute(value, "mp", [(source, source ^ flip) for source in range(4)])


def swapped_outer(value, flip):
    count = lax.axis_size(("frame", "mp"))
    return lax.ppermute(value, ("frame", "mp"), [(s, s ^ flip) for s in range(count)])


def dot(left, right):
    return jnp.dot(left, right, preferred_element_type=F32)


def on_device(latents, levels, window_mask, level_table, w_qkv, gain_q, gain_k, w_out):
    space_count = lax.axis_size("space")
    rows = latents.shape[1]
    width = latents.shape[2]
    model_width = w_qkv.shape[0]
    head_size = gain_q.shape[1]
    mp_index = lax.axis_index("mp")
    space_index = lax.axis_index("space")

    own_mod = lax.dynamic_slice(
        level_table, (levels[0], 0, mp_index * width), (1, 3, width)
    )[0]

    features = latents[0].astype(F32)
    sums = jnp.stack([jnp.sum(features, -1), jnp.sum(features * features, -1)])
    sums = sums + swapped(sums, 1) + swapped(sums, 2) + swapped(sums, 3)
    average = sums[0] / model_width
    spread = sums[1] / model_width - average * average
    normed = (
        (features - average[:, None]) * lax.rsqrt(spread + EPS)[:, None] * (1.0 + own_mod[1])
        + own_mod[0]
    ).astype(BF16)

    blocks = w_qkv[:, 0, :].reshape(4, width, 3 * head_size)

    def feature_block(flip):
        return lax.dynamic_index_in_dim(blocks, mp_index ^ flip, 0, keepdims=False)

    w_mine = jnp.concatenate([feature_block(0), feature_block(2)])
    w_other = swapped(jnp.concatenate([feature_block(1), feature_block(3)]), 1)

    out_blocks = w_out[0].reshape(head_size, 4, width)

    def out_block(flip):
        return lax.dynamic_index_in_dim(out_blocks, mp_index ^ flip, 1, keepdims=False)

    w_out_rows = jnp.concatenate(
        [
            out_block(0),
            swapped(out_block(1), 1),
            swapped_outer(out_block(2), 6),
            swapped_outer(out_block(3), 7),
        ]
    )

    partner = swapped(normed, 2)
    right = {0: (normed, partner)}
    left = {0: (normed, partner)}
    half = space_count // 2
    for k in range(1, half + 1):
        right[k] = (
            shifted(right[k - 1][0], "space", 1),
            shifted(right[k - 1][1], "space", 1) if k < half else None,
        )
        left[k] = (
            shifted(left[k - 1][0], "space", -1) if k < half else None,
            shifted(left[k - 1][1], "space", -1),
        )
    arrived = {0: [right[0]]}
    for k in range(1, half):
        arrived[k] = [right[k], left[k]]
    arrived[half] = [(right[half][0], left[half][1])]
    groups = [[0]] + [[-k, k] for k in range(1, half)] + [[half]]

    queries, contexts = [], []
    for k in range(half + 1):
        first = jnp.concatenate([pair[0] for pair in arrived[k]])
        second = jnp.concatenate([pair[1] for pair in arrived[k]])
        tokens = jnp.concatenate([first, second], axis=1)
        received = swapped(dot(tokens, w_other), 1)
        mixed = dot(tokens, w_mine) + received
        query = mixed[:, :head_size]
        keyed = mixed[:, head_size : 2 * head_size]
        query = (
            query * lax.rsqrt(jnp.mean(query * query, -1, keepdims=True) + EPS) * gain_q[0]
        ).astype(BF16)
        keyed = (
            keyed * lax.rsqrt(jnp.mean(keyed * keyed, -1, keepdims=True) + EPS) * gain_k[0]
        ).astype(BF16)
        key_value = jnp.concatenate([keyed, mixed[:, 2 * head_size :].astype(BF16)], axis=1)
        queries.append(query)
        contexts.append((key_value, shifted(key_value, "frame", 1), shifted(key_value, "frame", 2)))

    order = [offset for group in groups for offset in group]
    mask_blocks = window_mask[0].reshape(3, space_count, rows).astype(F32)
    allowed = [
        lax.dynamic_index_in_dim(
            mask_blocks, lax.rem(space_index + offset + space_count, space_count), 1, keepdims=False
        )
        for offset in order
    ]
    allowed = jnp.concatenate(allowed, axis=1)

    query = jnp.concatenate(queries)
    total = 0.0
    weighted = 0.0
    for back in (0, 2, 1):
        context = jnp.concatenate([c[back] for c in contexts])
        scores = lax.dot_general(
            query, context[:, :head_size], (((1,), (1,)), ((), ())), preferred_element_type=F32
        ) / math.sqrt(head_size)
        expo = jnp.exp(scores) * allowed[back][None, :]
        total = total + jnp.sum(expo, axis=1, keepdims=True)
        weighted = weighted + dot(expo.astype(BF16), context[:, head_size:])
    attended = (weighted / total).astype(BF16)

    near = swapped(attended, 1)
    across = swapped(attended, 2)
    across_near = swapped(across, 1)
    heads = jnp.concatenate([attended, near, across, across_near], axis=1)

    place = {offset: index for index, offset in enumerate(order)}

    def term(offset, columns=slice(None)):
        start = place[offset] * rows
        return dot(heads[start : start + rows], w_out_rows[:, columns])

    split = width // 2
    go_right = shifted(term(half, slice(0, split)).astype(BF16), "space", 1)
    go_left = shifted(term(half, slice(split, None)).astype(BF16), "space", -1)
    for k in range(half - 1, 0, -1):
        to_right, to_left = term(k), term(-k)
        if k == half - 1:
            to_right = jnp.concatenate(
                [to_right[:, :split] + go_right.astype(F32), to_right[:, split:]], axis=1
            )
            to_left = jnp.concatenate(
                [to_left[:, :split], to_left[:, split:] + go_left.astype(F32)], axis=1
            )
        else:
            to_right = to_right + go_right.astype(F32)
            to_left = to_left + go_left.astype(F32)
        go_right = shifted(to_right.astype(BF16), "space", 1)
        go_left = shifted(to_left.astype(BF16), "space", -1)
    branch_sum = term(0) + go_right.astype(F32) + go_left.astype(F32)
    return (features + own_mod[2] * branch_sum).astype(BF16)[None]


def solution(mesh):
    in_specs = (
        P("frame", "space", "mp"),
        P("frame"),
        P("frame", None, None),
        P(),
        P(None, ("space", "mp"), None),
        P(("space", "mp"), None),
        P(("space", "mp"), None),
        P(("space", "mp"), None, None),
    )
    out_specs = P("frame", "space", "mp")
    return jax.shard_map(
        on_device, mesh=mesh, in_specs=in_specs, out_specs=out_specs, check_vma=False
    )
```

```python
import functools
import math

import jax
import jax.numpy as jnp
import numpy as np
from jax import lax
from jax.experimental import pallas as pl
from jax.experimental.pallas import tpu as pltpu
from jax.sharding import PartitionSpec as P

EPS = 1e-06
BF16 = jnp.bfloat16
F32 = jnp.float32
SPACE = 8
STEPS = SPACE // 2


def shifted(value, steps):
    count = lax.axis_size("frame")
    pairs = [(source, (source + steps) % count) for source in range(count)]
    return lax.ppermute(value, "frame", pairs)


def swapped(value, flip):
    return lax.ppermute(value, "mp", [(source, source ^ flip) for source in range(4)])


def swapped_chips(value):
    count = lax.axis_size(("frame", "mp"))
    return lax.ppermute(value, ("frame", "mp"), [(s, s ^ (2 + s % 2 * 4)) for s in range(count)])


def onward(value):
    pairs = []
    for place in range(SPACE):
        for member in range(4):
            step = 1 if member % 2 == 0 else -1
            pairs.append((place * 4 + member, (place + step) % SPACE * 4 + member))
    return lax.ppermute(value, ("space", "mp"), pairs)


def after(value, *others):
    return lax.optimization_barrier((value,) + others)[0]


def dot(left, right):
    return jnp.dot(left, right, preferred_element_type=F32)


def rms_scaled(value, gain):
    return (value * lax.rsqrt(jnp.mean(value * value, -1, keepdims=True) + EPS) * gain).astype(BF16)


def project_kernel(counts, carried, chip_ref, mod_ref, gain_ref, w_ref, *refs):
    carry, refs = refs[:carried], refs[carried:]
    pieces = [(refs[2 * i], refs[2 * i + 1]) for i in range(len(counts))]
    query_ref, context_ref, token_ref, normed_ref = refs[-4:]
    side = pieces[0][0].shape[1]
    head_size = query_ref.shape[1]
    start_a = pl.multiple_of(chip_ref[0] * side, 128)
    start_b = pl.multiple_of((1 - chip_ref[0]) * side, 128)
    lanes = 128
    first = 0
    for (a_ref, b_ref), count in zip(pieces, counts):

        def tile(index, _, a_ref=a_ref, b_ref=b_ref, first=first):
            rows = [pl.ds(pl.multiple_of(index * 48 + 16 * group, 16), 16) for group in range(3)]
            sums = [jnp.zeros((16, lanes), F32)] * 3
            squares = [jnp.zeros((16, lanes), F32)] * 3
            for ref in (a_ref, b_ref):
                for column in range(0, side, lanes):
                    for group in range(3):
                        block = ref[rows[group], column : column + lanes].astype(F32)
                        sums[group] = sums[group] + block
                        squares[group] = squares[group] + block * block
            averages, inverses = [], []
            for group in range(3):
                average = jnp.sum(sums[group], -1, keepdims=True) / (2 * side)
                square = jnp.sum(squares[group], -1, keepdims=True) / (2 * side)
                inverse = lax.rsqrt(square - average * average + EPS)
                averages.append(jnp.broadcast_to(average, (16, lanes)))
                inverses.append(jnp.broadcast_to(inverse, (16, lanes)))
            for ref, start, offset in ((a_ref, start_a, 0), (b_ref, start_b, side)):
                for column in range(0, side, lanes):
                    where = pl.ds(pl.multiple_of(start + column, lanes), lanes)
                    scale = jnp.broadcast_to(mod_ref[1:2, where], (16, lanes))
                    shift = jnp.broadcast_to(mod_ref[0:1, where], (16, lanes))
                    for group in range(3):
                        block = ref[rows[group], column : column + lanes].astype(F32)
                        scaled = (block - averages[group]) * inverses[group] * scale + shift
                        place = pl.ds(pl.multiple_of(first + index * 48 + 16 * group, 16), 16)
                        normed_ref[place, offset + column : offset + column + lanes] = scaled.astype(BF16)
            return 0

        lax.fori_loop(0, count // 48, tile, 0)
        first += count
    mixed = dot(normed_ref[:, :side], w_ref[pl.ds(start_a, side), :]) + dot(
        normed_ref[:, side:], w_ref[pl.ds(start_b, side), :]
    )
    token_ref[...] = jnp.zeros_like(token_ref)
    begin = query_ref.shape[0] - first
    if carried:
        query_ref[:begin, :] = carry[0][...]
        context_ref[:begin, :] = carry[1][...]
    query_ref[begin:, :] = rms_scaled(mixed[:, :head_size], gain_ref[0:1, :])
    context_ref[begin:, :head_size] = rms_scaled(mixed[:, head_size : 2 * head_size], gain_ref[1:2, :])
    context_ref[begin:, head_size:] = mixed[:, 2 * head_size :].astype(BF16)


def project(chip, modulation, gains, weights, pieces, carry=(), following=()):
    counts = tuple(a.shape[0] for a, _ in pieces)
    total = sum(counts)
    features, columns = weights.shape
    head_size = gains.shape[1]
    out_rows = total + (carry[0].shape[0] if carry else 0)
    vmem, anywhere = pl.BlockSpec(memory_space=pltpu.VMEM), pl.BlockSpec(memory_space=pl.ANY)
    return pl.pallas_call(
        functools.partial(project_kernel, counts, len(carry)),
        out_shape=(
            jax.ShapeDtypeStruct((out_rows, head_size), BF16),
            jax.ShapeDtypeStruct((out_rows, 2 * head_size), BF16),
            jax.ShapeDtypeStruct((8, 128), F32),
        ),
        in_specs=[pl.BlockSpec(memory_space=pltpu.SMEM)]
        + [vmem] * (3 + len(carry) + 2 * len(pieces))
        + [anywhere] * len(following),
        out_specs=(vmem, vmem, vmem),
        scratch_shapes=[pltpu.VMEM((total, features), BF16)],
        compiler_params=pltpu.CompilerParams(vmem_limit_bytes=24 * 1024 * 1024),
        cost_estimate=pl.CostEstimate(flops=1024, bytes_accessed=1024, transcendentals=0),
        name="project",
    )(
        chip.reshape(1),
        modulation,
        gains,
        weights,
        *carry,
        *[part for pair in pieces for part in pair],
        *following,
    )


def masked_values(context, allowed):
    head_size = context.shape[1] // 2
    allowed = jnp.broadcast_to(allowed, (context.shape[0], head_size))
    values = context[:, head_size:].astype(F32) * allowed
    return jnp.concatenate([values, allowed], axis=1).astype(BF16)


def weighted_sums(query, key_ref, value_ref, chunks):
    scale = math.log2(math.e) / math.sqrt(query.shape[1])
    size = key_ref.shape[0] // chunks
    total = None
    for begin in range(0, key_ref.shape[0], size):
        scores = lax.dot_general(
            query, key_ref[begin : begin + size, :], (((1,), (1,)), ((), ())), preferred_element_type=F32
        )
        term = dot(jnp.exp2(scores * scale).astype(BF16), value_ref[begin : begin + size, :])
        total = term if total is None else total + term
    return total


def early_kernel(keys, core_ref, allowed_ref, *refs):
    queries, contexts = refs[:3], refs[3 : 3 + len(keys)]
    query_ref, sums_ref, key_ref, value_ref = refs[3 + len(keys) :]
    first, second, third = queries
    rows = second.shape[0] // 2
    half = rows // 2
    query_ref[0:rows, :] = first[rows : 2 * rows, :]
    query_ref[rows : 2 * rows, :] = second[:rows, :]
    query_ref[2 * rows : 3 * rows, :] = third[:rows, :]
    query_ref[3 * rows : 4 * rows, :] = first[:rows, :]
    flip = core_ref[0] * half
    query_ref[pl.ds(pl.multiple_of(4 * rows + flip, 16), half), :] = third[2 * rows : 2 * rows + half, :]
    query_ref[pl.ds(pl.multiple_of(4 * rows + half - flip, 16), half), :] = third[2 * rows + half :, :]
    query_ref[5 * rows : 6 * rows, :] = first[2 * rows :, :]
    query_ref[6 * rows : 7 * rows, :] = second[rows:, :]
    query_ref[7 * rows :, :] = third[rows : 2 * rows, :]

    begin = 0
    for (place, back), context in zip(keys, contexts):
        span = slice(begin, begin + context.shape[0])
        allowed = allowed_ref[place : place + context.shape[0], back : back + 1]
        key_ref[span, :] = context[:, : key_ref.shape[1]]
        value_ref[span, :] = masked_values(context, allowed)
        begin += context.shape[0]

    def tile(index, _):
        part = pl.ds(pl.multiple_of(index * 256, 256), 256)
        sums_ref[part, :] = weighted_sums(query_ref[part, :], key_ref, value_ref, 4)
        return 0

    lax.fori_loop(0, query_ref.shape[0] // 256, tile, 0)


def late_kernel(
    place, allowed_ref, query_ref, sums_ref, one_ref, two_ref, same_ref, other_ref, *scratch
):
    key_ref, value_ref, attended_ref = scratch
    count, head_size = query_ref.shape
    rows = count // 8
    size = one_ref.shape[0]
    for back, context in ((1, one_ref), (2, two_ref)):
        span = slice((back - 1) * size, back * size)
        allowed = allowed_ref[place : place + size, back : back + 1]
        key_ref[span, :] = context[:, :head_size]
        value_ref[span, :] = masked_values(context, allowed)

    def tile(index, _):
        part = pl.ds(pl.multiple_of(index * 256, 256), 256)
        sums = sums_ref[part, :] + weighted_sums(query_ref[part, :], key_ref, value_ref, 1)
        attended_ref[part, :] = (sums[:, :head_size] / sums[:, head_size:]).astype(BF16)
        return 0

    lax.fori_loop(0, count // 256, tile, 0)
    other_ref[...] = attended_ref[: 5 * rows, :]
    same_ref[...] = attended_ref[3 * rows :, :]


def term_kernel(steps, core_ref, same_ref, far_ref, near_ref, opposite_ref, w_ref, w_other_ref, *outs):
    width = w_ref.shape[1] // 2
    rows = same_ref.shape[0] // 5
    for (step, side, _), out_ref in zip(steps, outs):
        start = (0 if step == 0 else 1 if step == STEPS else 1 + step) * rows
        begin = (start - 2 * rows) % (5 * rows)
        place = core_ref[0] if side == 0 else 1 - core_ref[0]
        columns = pl.ds(pl.multiple_of(place * width, 128), width)
        same = jnp.concatenate([same_ref[start : start + rows], far_ref[start : start + rows]], axis=1)
        other = jnp.concatenate(
            [near_ref[begin : begin + rows], opposite_ref[begin : begin + rows]], axis=1
        )
        term = dot(same, w_ref[:, columns]) + dot(other, w_other_ref[:, columns])
        out_ref[...] = term.astype(out_ref.dtype)


def vmem_call(kernel, out_shape, *operands, scalars=0, scratch=()):
    vmem = pl.BlockSpec(memory_space=pltpu.VMEM)
    return pl.pallas_call(
        kernel,
        out_shape=out_shape,
        in_specs=[pl.BlockSpec(memory_space=pltpu.SMEM)] * scalars + [vmem] * (len(operands) - scalars),
        out_specs=tuple([vmem] * len(out_shape)),
        scratch_shapes=scratch,
        compiler_params=pltpu.CompilerParams(vmem_limit_bytes=20 * 1024 * 1024),
        cost_estimate=pl.CostEstimate(flops=1024, bytes_accessed=1024, transcendentals=0),
        name="attend",
    )(*operands)


def on_device(latents, levels, window_mask, level_table, w_qkv, gain_q, gain_k, w_out):
    rows = latents.shape[1]
    width = latents.shape[2]
    model_width = w_qkv.shape[0]
    head_size = gain_q.shape[1]
    half = rows // 2
    mp_index = lax.axis_index("mp")
    space_index = lax.axis_index("space")
    core = lax.rem(mp_index, 2)
    chip = mp_index // 2

    own = latents[0]
    with jax.named_scope("own_rows_near"):
        near = swapped(own, 1)
    with jax.named_scope("own_rows_far"):
        far = swapped(own, 2)
    def in_core_order(mine, other):
        return jnp.concatenate([jnp.where(core == 0, mine, other), jnp.where(core == 0, other, mine)], axis=1)

    def ring(name, value):
        with jax.named_scope(name):
            return onward(value)

    def both(name, first, second):
        with jax.named_scope(name):
            return (first, second), (swapped(first, 1), swapped(second, 1))

    def core_half(block):
        return lax.dynamic_slice_in_dim(block, core * half, half, 0)

    a_0 = in_core_order(own, near)
    a_1 = ring("ring_a1", a_0)
    with jax.named_scope("own_rows_far_near"):
        far_near = swapped(after(far, a_1), 1)
    b_0 = in_core_order(far, far_near)
    b_1 = ring("ring_b1", b_0)

    level = after(levels, a_1)[0]
    own_mod = lax.dynamic_slice(level_table, (level, 0, 0), (1, 3, model_width))[0]
    gate = lax.dynamic_slice_in_dim(own_mod[2], mp_index * width, width, 0)
    gains = jnp.concatenate([gain_q, gain_k])
    mod_rows = jnp.stack([own_mod[0], 1.0 + own_mod[1]])

    def projected(*pieces, carry=(), following=()):
        return project(chip, mod_rows, gains, w_qkv[:, 0, :], pieces, carry, following)

    def with_prior(name, context):
        with jax.named_scope(name):
            return context, shifted(context, 1), shifted(context, 2)

    a_2 = ring("ring_a2", a_1)
    *carry, done_0 = projected((a_0, b_0))
    b_2 = ring("ring_b2", after(b_1, done_0))
    a_3 = ring("ring_a3", a_2)
    query_01, context_01, done_01 = projected(*both("rows_1", a_1, b_1), carry=carry, following=(a_2,))
    contexts = [with_prior("prior_01", context_01)]
    b_3 = ring("ring_b3", after(b_2, done_01))
    a_4 = ring("ring_a4", core_half(a_3))
    query_2, context_2, done_2 = projected(*both("rows_2", a_2, b_2), following=(a_3, done_01))
    contexts.append(with_prior("prior_2", context_2))
    b_4 = ring("ring_b4", after(core_half(b_3), done_2))
    query_3, context_3, _ = projected(
        *both("rows_3", a_3, b_3), *both("rows_4", a_4, b_4), following=(done_2, *contexts[0][1:])
    )
    contexts.append(with_prior("prior_3", context_3))

    def chip_columns(source, index):
        return lax.dynamic_slice_in_dim(source, index * 2 * width, 2 * width, 1)

    w_out_own = after(w_out[0], done_0)
    with jax.named_scope("out_weights_far"):
        out_far = swapped_chips(chip_columns(w_out_own, 1 - chip))
    out_rows = jnp.concatenate([chip_columns(w_out_own, chip), out_far])
    with jax.named_scope("out_weights_near"):
        out_other_rows = swapped(out_rows, 1)

    hop = [0] * rows + [sign * step for step in range(1, STEPS) for sign in (-1, 1) for _ in range(rows)]
    hop += [-STEPS] * half + [STEPS] * half
    within = list(range(rows)) * (2 * STEPS - 1) + list(range(half)) * 2
    first_half = [0] * (len(hop) - rows) + [1] * half + [-1] * half
    hop, within, first_half = (np.asarray(v, np.int32) for v in (hop, within, first_half))
    mask, here = after(window_mask[0], a_3), after(space_index, a_3)
    block = (here + hop * (1 - 2 * core) + SPACE) % SPACE
    extra = jnp.where(first_half == 0, 0, jnp.where(first_half > 0, core, 1 - core)) * half
    order = block * rows + within + extra
    pick = (order[:, None] == jnp.arange(rows * SPACE, dtype=jnp.int32)[None, :]).astype(BF16)
    allowed = lax.dot_general(
        pick, mask.astype(BF16), (((1,), (1,)), ((), ())), preferred_element_type=F32
    )

    keys, parts, begin = [], [], 0
    for context in contexts[:-1]:
        for back in range(3):
            keys.append((begin, back))
            parts.append(context[back])
        begin += context[0].shape[0]
    keys.append((begin, 0))
    parts.append(contexts[-1][0])
    count, last = rows * SPACE, contexts[-1][0].shape[0]
    early = sum(part.shape[0] for part in parts)

    def key_scratch(size):
        return [pltpu.VMEM((size, head_size), BF16), pltpu.VMEM((size, 2 * head_size), BF16)]

    query, sums = vmem_call(
        functools.partial(early_kernel, tuple(keys)),
        (
            jax.ShapeDtypeStruct((count, head_size), BF16),
            jax.ShapeDtypeStruct((count, 2 * head_size), F32),
        ),
        core.reshape(1),
        allowed,
        query_01,
        query_2,
        query_3,
        *parts,
        scalars=1,
        scratch=key_scratch(early),
    )
    for_same, for_other = vmem_call(
        functools.partial(late_kernel, begin),
        (jax.ShapeDtypeStruct((5 * rows, head_size), BF16),) * 2,
        allowed,
        query,
        sums,
        *contexts[-1][1:],
        scratch=key_scratch(2 * last) + [pltpu.VMEM((count, head_size), BF16)],
    )
    with jax.named_scope("heads"):
        far_heads = swapped(for_same, 2)
        near_heads, opposite_heads = swapped(for_other, 1), swapped(for_other, 3)

    def terms(steps):
        return vmem_call(
            functools.partial(term_kernel, steps),
            tuple(jax.ShapeDtypeStruct((rows, width), BF16 if wide < 0 else F32) for _, _, wide in steps),
            core.reshape(1),
            for_same,
            far_heads,
            near_heads,
            opposite_heads,
            out_rows,
            out_other_rows,
            scalars=1,
        )

    first_a, first_b = terms(((STEPS, 0, -1), (STEPS - 1, 1, -1)))
    sum_a = ring("sum_a4", first_a)
    sum_b = ring("sum_b3", first_b)
    order = [(k, side) for k in range(STEPS - 1, 0, -1) for side in (0, 1) if (k, side) != (STEPS - 1, 1)]
    rest = dict(zip(order + [(0, 0)], terms(tuple((k, side, 1) for k, side in order + [(0, 0)]))))
    for k in range(STEPS - 1, 0, -1):
        sum_a = ring(f"sum_a{k}", (rest[k, 0] + sum_a.astype(F32)).astype(BF16))
        if k > 1:
            sum_b = ring(f"sum_b{k - 1}", (rest[k - 1, 1] + sum_b.astype(F32)).astype(BF16))
    branch_sum = rest[0, 0] + sum_a.astype(F32) + swapped(sum_b, 1).astype(F32)
    return (own.astype(F32) + gate * branch_sum).astype(BF16)[None]


def solution(mesh):
    in_specs = (
        P("frame", "space", "mp"),
        P("frame"),
        P("frame", None, None),
        P(),
        P(None, ("space", "mp"), None),
        P(("space", "mp"), None),
        P(("space", "mp"), None),
        P(("space", "mp"), None, None),
    )
    out_specs = P("frame", "space", "mp")
    return jax.shard_map(
        on_device, mesh=mesh, in_specs=in_specs, out_specs=out_specs, check_vma=False
    )
```

```python
import functools
import math

import jax
import jax.numpy as jnp
import numpy as np
from jax import lax
from jax.experimental import pallas as pl
from jax.experimental.pallas import tpu as pltpu
from jax.sharding import PartitionSpec as P

EPS = 1e-06
BF16 = jnp.bfloat16
F32 = jnp.float32
SPACE = 8
STEPS = SPACE // 2


def shifted(value, steps):
    count = lax.axis_size("frame")
    pairs = [(source, (source + steps) % count) for source in range(count)]
    return lax.ppermute(value, "frame", pairs)


def swapped(value, flip):
    return lax.ppermute(value, "mp", [(source, source ^ flip) for source in range(4)])


def swapped_chips(value):
    count = lax.axis_size(("frame", "mp"))
    return lax.ppermute(value, ("frame", "mp"), [(s, s ^ (2 + s % 2 * 4)) for s in range(count)])


def onward(value):
    pairs = []
    for place in range(SPACE):
        for member in range(4):
            step = 1 if member % 2 == 0 else -1
            pairs.append((place * 4 + member, (place + step) % SPACE * 4 + member))
    return lax.ppermute(value, ("space", "mp"), pairs)


def after(value, *others):
    return lax.optimization_barrier((value,) + others)[0]


def dot(left, right):
    return jnp.dot(left, right, preferred_element_type=F32)


def rms_scaled(value, gain):
    return (value * lax.rsqrt(jnp.mean(value * value, -1, keepdims=True) + EPS) * gain).astype(BF16)


def project_kernel(counts, carried, chip_ref, mod_ref, gain_ref, w_ref, *refs):
    carry, refs = refs[:carried], refs[carried:]
    pieces = [(refs[2 * i], refs[2 * i + 1]) for i in range(len(counts))]
    query_ref, context_ref, token_ref, normed_ref = refs[-4:]
    side = pieces[0][0].shape[1]
    head_size = query_ref.shape[1]
    start_a = pl.multiple_of(chip_ref[0] * side, 128)
    start_b = pl.multiple_of((1 - chip_ref[0]) * side, 128)
    lanes = 128
    first = 0
    for (a_ref, b_ref), count in zip(pieces, counts):

        def tile(index, _, a_ref=a_ref, b_ref=b_ref, first=first):
            rows = [pl.ds(pl.multiple_of(index * 48 + 16 * group, 16), 16) for group in range(3)]
            sums = [jnp.zeros((16, lanes), F32)] * 3
            squares = [jnp.zeros((16, lanes), F32)] * 3
            for ref in (a_ref, b_ref):
                for column in range(0, side, lanes):
                    for group in range(3):
                        block = ref[rows[group], column : column + lanes].astype(F32)
                        sums[group] = sums[group] + block
                        squares[group] = squares[group] + block * block
            averages, inverses = [], []
            for group in range(3):
                average = jnp.sum(sums[group], -1, keepdims=True) / (2 * side)
                square = jnp.sum(squares[group], -1, keepdims=True) / (2 * side)
                inverse = lax.rsqrt(square - average * average + EPS)
                averages.append(jnp.broadcast_to(average, (16, lanes)))
                inverses.append(jnp.broadcast_to(inverse, (16, lanes)))
            for ref, start, offset in ((a_ref, start_a, 0), (b_ref, start_b, side)):
                for column in range(0, side, lanes):
                    where = pl.ds(pl.multiple_of(start + column, lanes), lanes)
                    scale = jnp.broadcast_to(mod_ref[1:2, where], (16, lanes))
                    shift = jnp.broadcast_to(mod_ref[0:1, where], (16, lanes))
                    for group in range(3):
                        block = ref[rows[group], column : column + lanes].astype(F32)
                        scaled = (block - averages[group]) * inverses[group] * scale + shift
                        place = pl.ds(pl.multiple_of(first + index * 48 + 16 * group, 16), 16)
                        normed_ref[place, offset + column : offset + column + lanes] = scaled.astype(BF16)
            return 0

        lax.fori_loop(0, count // 48, tile, 0)
        first += count
    mixed = dot(normed_ref[:, :side], w_ref[pl.ds(start_a, side), :]) + dot(
        normed_ref[:, side:], w_ref[pl.ds(start_b, side), :]
    )
    token_ref[...] = jnp.zeros_like(token_ref)
    begin = query_ref.shape[0] - first
    if carried:
        query_ref[:begin, :] = carry[0][...]
        context_ref[:begin, :] = carry[1][...]
    query_ref[begin:, :] = rms_scaled(mixed[:, :head_size], gain_ref[0:1, :])
    context_ref[begin:, :head_size] = rms_scaled(mixed[:, head_size : 2 * head_size], gain_ref[1:2, :])
    context_ref[begin:, head_size:] = mixed[:, 2 * head_size :].astype(BF16)


def project(chip, modulation, gains, weights, pieces, carry=(), following=(), flops=1024):
    counts = tuple(a.shape[0] for a, _ in pieces)
    total = sum(counts)
    features, columns = weights.shape
    head_size = gains.shape[1]
    out_rows = total + (carry[0].shape[0] if carry else 0)
    vmem, anywhere = pl.BlockSpec(memory_space=pltpu.VMEM), pl.BlockSpec(memory_space=pl.ANY)
    return pl.pallas_call(
        functools.partial(project_kernel, counts, len(carry)),
        out_shape=(
            jax.ShapeDtypeStruct((out_rows, head_size), BF16),
            jax.ShapeDtypeStruct((out_rows, 2 * head_size), BF16),
            jax.ShapeDtypeStruct((8, 128), F32),
        ),
        in_specs=[pl.BlockSpec(memory_space=pltpu.SMEM)]
        + [vmem] * (3 + len(carry) + 2 * len(pieces))
        + [anywhere] * len(following),
        out_specs=(vmem, vmem, vmem),
        scratch_shapes=[pltpu.VMEM((total, features), BF16)],
        compiler_params=pltpu.CompilerParams(vmem_limit_bytes=16 * 1024 * 1024),
        cost_estimate=pl.CostEstimate(flops=flops, bytes_accessed=1024, transcendentals=0),
        name="project",
    )(
        chip.reshape(1),
        modulation,
        gains,
        weights,
        *carry,
        *[part for pair in pieces for part in pair],
        *following,
    )


def masked_values(context, allowed):
    head_size = context.shape[1] // 2
    allowed = jnp.broadcast_to(allowed, (context.shape[0], head_size))
    values = context[:, head_size:].astype(F32) * allowed
    return jnp.concatenate([values, allowed], axis=1).astype(BF16)


def weighted_sums(query, key_ref, value_ref, chunks):
    scale = math.log2(math.e) / math.sqrt(query.shape[1])
    size = key_ref.shape[0] // chunks
    total = None
    for begin in range(0, key_ref.shape[0], size):
        scores = lax.dot_general(
            query, key_ref[begin : begin + size, :], (((1,), (1,)), ((), ())), preferred_element_type=F32
        )
        term = dot(jnp.exp2(scores * scale).astype(BF16), value_ref[begin : begin + size, :])
        total = term if total is None else total + term
    return total


def early_kernel(keys, core_ref, allowed_ref, *refs):
    queries, contexts = refs[:3], refs[3 : 3 + len(keys)]
    query_ref, sums_ref, key_ref, value_ref = refs[3 + len(keys) :]
    first, second, third = queries
    rows = second.shape[0] // 2
    half = rows // 2
    query_ref[0:rows, :] = first[rows : 2 * rows, :]
    query_ref[rows : 2 * rows, :] = second[:rows, :]
    query_ref[2 * rows : 3 * rows, :] = third[:rows, :]
    query_ref[3 * rows : 4 * rows, :] = first[:rows, :]
    flip = core_ref[0] * half
    query_ref[pl.ds(pl.multiple_of(4 * rows + flip, 16), half), :] = third[2 * rows : 2 * rows + half, :]
    query_ref[pl.ds(pl.multiple_of(4 * rows + half - flip, 16), half), :] = third[2 * rows + half :, :]
    query_ref[5 * rows : 6 * rows, :] = first[2 * rows :, :]
    query_ref[6 * rows : 7 * rows, :] = second[rows:, :]
    query_ref[7 * rows :, :] = third[rows : 2 * rows, :]

    begin = 0
    for (place, back), context in zip(keys, contexts):
        span = slice(begin, begin + context.shape[0])
        allowed = allowed_ref[place : place + context.shape[0], back : back + 1]
        key_ref[span, :] = context[:, : key_ref.shape[1]]
        value_ref[span, :] = masked_values(context, allowed)
        begin += context.shape[0]

    def tile(index, _):
        part = pl.ds(pl.multiple_of(index * 256, 256), 256)
        sums_ref[part, :] = weighted_sums(query_ref[part, :], key_ref, value_ref, 4)
        return 0

    lax.fori_loop(0, query_ref.shape[0] // 256, tile, 0)


def late_kernel(
    place, allowed_ref, query_ref, sums_ref, one_ref, two_ref, same_ref, other_ref, *scratch
):
    key_ref, value_ref, attended_ref = scratch
    count, head_size = query_ref.shape
    rows = count // 8
    size = one_ref.shape[0]
    for back, context in ((1, one_ref), (2, two_ref)):
        span = slice((back - 1) * size, back * size)
        allowed = allowed_ref[place : place + size, back : back + 1]
        key_ref[span, :] = context[:, :head_size]
        value_ref[span, :] = masked_values(context, allowed)

    def tile(index, _):
        part = pl.ds(pl.multiple_of(index * 256, 256), 256)
        sums = sums_ref[part, :] + weighted_sums(query_ref[part, :], key_ref, value_ref, 1)
        attended_ref[part, :] = (sums[:, :head_size] / sums[:, head_size:]).astype(BF16)
        return 0

    lax.fori_loop(0, count // 256, tile, 0)
    other_ref[...] = attended_ref[: 5 * rows, :]
    same_ref[...] = attended_ref[3 * rows :, :]


def term_kernel(steps, core_ref, same_ref, far_ref, near_ref, opposite_ref, w_ref, w_other_ref, *outs):
    width = w_ref.shape[1] // 2
    rows = same_ref.shape[0] // 5
    for (step, side, _), out_ref in zip(steps, outs):
        start = (0 if step == 0 else 1 if step == STEPS else 1 + step) * rows
        begin = (start - 2 * rows) % (5 * rows)
        place = core_ref[0] if side == 0 else 1 - core_ref[0]
        columns = pl.ds(pl.multiple_of(place * width, 128), width)
        same = jnp.concatenate([same_ref[start : start + rows], far_ref[start : start + rows]], axis=1)
        other = jnp.concatenate(
            [near_ref[begin : begin + rows], opposite_ref[begin : begin + rows]], axis=1
        )
        term = dot(same, w_ref[:, columns]) + dot(other, w_other_ref[:, columns])
        out_ref[...] = term.astype(out_ref.dtype)


def vmem_call(kernel, out_shape, *operands, scalars=0, scratch=(), flops=1024):
    vmem = pl.BlockSpec(memory_space=pltpu.VMEM)
    return pl.pallas_call(
        kernel,
        out_shape=out_shape,
        in_specs=[pl.BlockSpec(memory_space=pltpu.SMEM)] * scalars + [vmem] * (len(operands) - scalars),
        out_specs=tuple([vmem] * len(out_shape)),
        scratch_shapes=scratch,
        compiler_params=pltpu.CompilerParams(vmem_limit_bytes=12 * 1024 * 1024),
        cost_estimate=pl.CostEstimate(flops=flops, bytes_accessed=1024, transcendentals=0),
        name="attend",
    )(*operands)


def on_device(latents, levels, window_mask, level_table, w_qkv, gain_q, gain_k, w_out):
    rows = latents.shape[1]
    width = latents.shape[2]
    model_width = w_qkv.shape[0]
    head_size = gain_q.shape[1]
    half = rows // 2
    mp_index = lax.axis_index("mp")
    space_index = lax.axis_index("space")
    core = lax.rem(mp_index, 2)
    chip = mp_index // 2

    own = latents[0]
    with jax.named_scope("own_rows_near"):
        near = swapped(own, 1)
    with jax.named_scope("own_rows_far"):
        far = swapped(own, 2)
    def in_core_order(mine, other):
        return jnp.concatenate([jnp.where(core == 0, mine, other), jnp.where(core == 0, other, mine)], axis=1)

    def ring(name, value):
        with jax.named_scope(name):
            return onward(value)

    def both(name, first, second):
        with jax.named_scope(name):
            return (first, second), (swapped(first, 1), swapped(second, 1))

    def core_half(block):
        return lax.dynamic_slice_in_dim(block, core * half, half, 0)

    a_0 = in_core_order(own, near)
    a_1 = ring("ring_a1", a_0)
    with jax.named_scope("own_rows_far_near"):
        far_near = swapped(after(far, a_1), 1)
    b_0 = in_core_order(far, far_near)
    b_1 = ring("ring_b1", b_0)

    level = after(levels, a_1)[0]
    own_mod = lax.dynamic_slice(level_table, (level, 0, 0), (1, 3, model_width))[0]
    gate = lax.dynamic_slice_in_dim(own_mod[2], mp_index * width, width, 0)
    gains = jnp.concatenate([gain_q, gain_k])
    mod_rows = jnp.stack([own_mod[0], 1.0 + own_mod[1]])

    w_own = w_qkv[:, 0, :]

    def projected(*pieces, carry=(), following=(), flops=1024):
        return project(chip, mod_rows, gains, w_own, pieces, carry, following, flops)

    def with_prior(name, context):
        with jax.named_scope(name):
            return context, shifted(context, 1), shifted(context, 2)

    a_2 = ring("ring_a2", a_1)
    b_2 = ring("ring_b2", b_1)
    a_3 = ring("ring_a3", a_2)
    query_01, context_01, done_01 = projected((a_0, b_0), *both("rows_1", a_1, b_1), following=(a_2,))
    contexts = [with_prior("prior_01", context_01)]
    b_3 = ring("ring_b3", after(b_2, done_01))
    a_4 = ring("ring_a4", core_half(a_3))
    b_4 = ring("ring_b4", core_half(b_3))
    def chip_columns(source, index):
        return lax.dynamic_slice_in_dim(source, index * 2 * width, 2 * width, 1)

    w_out_own = after(w_out[0], b_0)
    with jax.named_scope("out_weights_far"):
        out_far = swapped_chips(chip_columns(w_out_own, 1 - chip))
    out_rows = jnp.concatenate([chip_columns(w_out_own, chip), out_far])
    with jax.named_scope("out_weights_near"):
        out_other_rows = swapped(out_rows, 1)

    hop = [0] * rows + [sign * step for step in range(1, STEPS) for sign in (-1, 1) for _ in range(rows)]
    hop += [-STEPS] * half + [STEPS] * half
    within = list(range(rows)) * (2 * STEPS - 1) + list(range(half)) * 2
    first_half = [0] * (len(hop) - rows) + [1] * half + [-1] * half
    hop, within, first_half = (np.asarray(v, np.int32) for v in (hop, within, first_half))
    mask, here = after(window_mask[0], b_1), after(space_index, b_1)
    block = (here + hop * (1 - 2 * core) + SPACE) % SPACE
    extra = jnp.where(first_half == 0, 0, jnp.where(first_half > 0, core, 1 - core)) * half
    order = block * rows + within + extra
    pick = (order[:, None] == jnp.arange(rows * SPACE, dtype=jnp.int32)[None, :]).astype(BF16)
    allowed = lax.dot_general(
        pick, mask.astype(BF16), (((1,), (1,)), ((), ())), preferred_element_type=F32
    )

    query_2, context_2, done_2 = projected(*both("rows_2", a_2, b_2), following=(a_3, done_01, out_other_rows, allowed, *contexts[0][1:]))
    contexts.append(with_prior("prior_2", context_2))
    query_3, context_3, _ = projected(
        *both("rows_3", after(a_3, done_2), after(b_3, done_2)),
        *both("rows_4", a_4, b_4),
        following=(done_2,),
        flops=10**10,
    )
    contexts.append(with_prior("prior_3", context_3))

    keys, parts, begin = [], [], 0
    for context in contexts[:-1]:
        for back in range(3):
            keys.append((begin, back))
            parts.append(context[back])
        begin += context[0].shape[0]
    keys.append((begin, 0))
    parts.append(contexts[-1][0])
    count, last = rows * SPACE, contexts[-1][0].shape[0]
    early = sum(part.shape[0] for part in parts)

    def key_scratch(size):
        return [pltpu.VMEM((size, head_size), BF16), pltpu.VMEM((size, 2 * head_size), BF16)]

    query, sums = vmem_call(
        functools.partial(early_kernel, tuple(keys)),
        (
            jax.ShapeDtypeStruct((count, head_size), BF16),
            jax.ShapeDtypeStruct((count, 2 * head_size), F32),
        ),
        core.reshape(1),
        allowed,
        query_01,
        query_2,
        query_3,
        *parts,
        scalars=1,
        scratch=key_scratch(early),
        flops=10**10,
    )
    for_same, for_other = vmem_call(
        functools.partial(late_kernel, begin),
        (jax.ShapeDtypeStruct((5 * rows, head_size), BF16),) * 2,
        allowed,
        query,
        sums,
        *contexts[-1][1:],
        scratch=key_scratch(2 * last) + [pltpu.VMEM((count, head_size), BF16)],
    )
    with jax.named_scope("heads"):
        far_heads = swapped(for_same, 2)
        near_heads, opposite_heads = swapped(for_other, 1), swapped(for_other, 3)

    def terms(steps):
        return vmem_call(
            functools.partial(term_kernel, steps),
            tuple(jax.ShapeDtypeStruct((rows, width), BF16 if wide < 0 else F32) for _, _, wide in steps),
            core.reshape(1),
            for_same,
            far_heads,
            near_heads,
            opposite_heads,
            out_rows,
            out_other_rows,
            scalars=1,
        )

    first_b, first_a = terms(((STEPS - 1, 1, -1), (STEPS, 0, -1)))
    sum_b = ring("sum_b3", first_b)
    sum_a = ring("sum_a4", first_a)
    order = [(k, side) for k in range(STEPS - 1, 0, -1) for side in (0, 1) if (k, side) != (STEPS - 1, 1)]
    rest = dict(zip(order + [(0, 0)], terms(tuple((k, side, 1) for k, side in order + [(0, 0)]))))
    for k in range(STEPS - 1, 0, -1):
        if k > 1:
            sum_b = ring(f"sum_b{k - 1}", (rest[k - 1, 1] + sum_b.astype(F32)).astype(BF16))
        sum_a = ring(f"sum_a{k}", (rest[k, 0] + sum_a.astype(F32)).astype(BF16))
    branch_sum = rest[0, 0] + (swapped(sum_b, 1).astype(F32) + sum_a.astype(F32))
    return (own.astype(F32) + gate * branch_sum).astype(BF16)[None]


def solution(mesh):
    in_specs = (
        P("frame", "space", "mp"),
        P("frame"),
        P("frame", None, None),
        P(),
        P(None, ("space", "mp"), None),
        P(("space", "mp"), None),
        P(("space", "mp"), None),
        P(("space", "mp"), None, None),
    )
    out_specs = P("frame", "space", "mp")
    return jax.shard_map(
        on_device, mesh=mesh, in_specs=in_specs, out_specs=out_specs, check_vma=False
    )
```

```python
import functools
import math

import jax
import jax.numpy as jnp
import numpy as np
from jax import lax
from jax.experimental import pallas as pl
from jax.experimental.pallas import tpu as pltpu
from jax.sharding import PartitionSpec as P

EPS = 1e-06
BF16 = jnp.bfloat16
F32 = jnp.float32
SPACE = 8
STEPS = SPACE // 2


def shifted(value, steps):
    count = lax.axis_size("frame")
    pairs = [(source, (source + steps) % count) for source in range(count)]
    return lax.ppermute(value, "frame", pairs)


def swapped(value, flip):
    return lax.ppermute(value, "mp", [(source, source ^ flip) for source in range(4)])


def swapped_chips(value):
    count = lax.axis_size(("frame", "mp"))
    return lax.ppermute(value, ("frame", "mp"), [(s, s ^ (2 + s % 2 * 4)) for s in range(count)])


def onward(value):
    pairs = []
    for place in range(SPACE):
        for member in range(4):
            step = 1 if member % 2 == 0 else -1
            pairs.append((place * 4 + member, (place + step) % SPACE * 4 + member))
    return lax.ppermute(value, ("space", "mp"), pairs)


def after(value, *others):
    return lax.optimization_barrier((value,) + others)[0]


def dot(left, right):
    return jnp.dot(left, right, preferred_element_type=F32)


def rms_scaled(value, gain):
    return (value * lax.rsqrt(jnp.mean(value * value, -1, keepdims=True) + EPS) * gain).astype(BF16)


def project_kernel(counts, carried, chip_ref, mod_ref, gain_ref, w_ref, *refs):
    carry, refs = refs[:carried], refs[carried:]
    pieces = [(refs[2 * i], refs[2 * i + 1]) for i in range(len(counts))]
    query_ref, context_ref, token_ref, normed_ref = refs[-4:]
    side = pieces[0][0].shape[1]
    head_size = query_ref.shape[1]
    start_a = pl.multiple_of(chip_ref[0] * side, 128)
    start_b = pl.multiple_of((1 - chip_ref[0]) * side, 128)
    lanes = 128
    first = 0
    for (a_ref, b_ref), count in zip(pieces, counts):

        def tile(index, _, a_ref=a_ref, b_ref=b_ref, first=first):
            rows = [pl.ds(pl.multiple_of(index * 48 + 16 * group, 16), 16) for group in range(3)]
            sums = [jnp.zeros((16, lanes), F32)] * 3
            squares = [jnp.zeros((16, lanes), F32)] * 3
            for ref in (a_ref, b_ref):
                for column in range(0, side, lanes):
                    for group in range(3):
                        block = ref[rows[group], column : column + lanes].astype(F32)
                        sums[group] = sums[group] + block
                        squares[group] = squares[group] + block * block
            averages, inverses = [], []
            for group in range(3):
                average = jnp.sum(sums[group], -1, keepdims=True) / (2 * side)
                square = jnp.sum(squares[group], -1, keepdims=True) / (2 * side)
                inverse = lax.rsqrt(square - average * average + EPS)
                averages.append(jnp.broadcast_to(average, (16, lanes)))
                inverses.append(jnp.broadcast_to(inverse, (16, lanes)))
            for ref, start, offset in ((a_ref, start_a, 0), (b_ref, start_b, side)):
                for column in range(0, side, lanes):
                    where = pl.ds(pl.multiple_of(start + column, lanes), lanes)
                    scale = jnp.broadcast_to(mod_ref[1:2, where], (16, lanes))
                    shift = jnp.broadcast_to(mod_ref[0:1, where], (16, lanes))
                    for group in range(3):
                        block = ref[rows[group], column : column + lanes].astype(F32)
                        scaled = (block - averages[group]) * inverses[group] * scale + shift
                        place = pl.ds(pl.multiple_of(first + index * 48 + 16 * group, 16), 16)
                        normed_ref[place, offset + column : offset + column + lanes] = scaled.astype(BF16)
            return 0

        lax.fori_loop(0, count // 48, tile, 0)
        first += count
    mixed = dot(normed_ref[:, :side], w_ref[pl.ds(start_a, side), :]) + dot(
        normed_ref[:, side:], w_ref[pl.ds(start_b, side), :]
    )
    token_ref[...] = jnp.zeros_like(token_ref)
    begin = query_ref.shape[0] - first
    if carried:
        query_ref[:begin, :] = carry[0][...]
        context_ref[:begin, :] = carry[1][...]
    query_ref[begin:, :] = rms_scaled(mixed[:, :head_size], gain_ref[0:1, :])
    context_ref[begin:, :head_size] = rms_scaled(mixed[:, head_size : 2 * head_size], gain_ref[1:2, :])
    context_ref[begin:, head_size:] = mixed[:, 2 * head_size :].astype(BF16)


def project(chip, modulation, gains, weights, pieces, carry=(), following=(), flops=1024):
    counts = tuple(a.shape[0] for a, _ in pieces)
    total = sum(counts)
    features, columns = weights.shape
    head_size = gains.shape[1]
    out_rows = total + (carry[0].shape[0] if carry else 0)
    vmem, anywhere = pl.BlockSpec(memory_space=pltpu.VMEM), pl.BlockSpec(memory_space=pl.ANY)
    return pl.pallas_call(
        functools.partial(project_kernel, counts, len(carry)),
        out_shape=(
            jax.ShapeDtypeStruct((out_rows, head_size), BF16),
            jax.ShapeDtypeStruct((out_rows, 2 * head_size), BF16),
            jax.ShapeDtypeStruct((8, 128), F32),
        ),
        in_specs=[pl.BlockSpec(memory_space=pltpu.SMEM)]
        + [vmem] * (3 + len(carry) + 2 * len(pieces))
        + [anywhere] * len(following),
        out_specs=(vmem, vmem, vmem),
        scratch_shapes=[pltpu.VMEM((total, features), BF16)],
        compiler_params=pltpu.CompilerParams(vmem_limit_bytes=16 * 1024 * 1024),
        cost_estimate=pl.CostEstimate(flops=flops, bytes_accessed=1024, transcendentals=0),
        name="project",
    )(
        chip.reshape(1),
        modulation,
        gains,
        weights,
        *carry,
        *[part for pair in pieces for part in pair],
        *following,
    )


def masked_values(context, allowed):
    head_size = context.shape[1] // 2
    allowed = jnp.broadcast_to(allowed, (context.shape[0], head_size))
    values = context[:, head_size:].astype(F32) * allowed
    return jnp.concatenate([values, allowed], axis=1).astype(BF16)


def weighted_sums(query, key_ref, value_ref, chunks):
    scale = math.log2(math.e) / math.sqrt(query.shape[1])
    size = key_ref.shape[0] // chunks
    total = None
    for begin in range(0, key_ref.shape[0], size):
        scores = lax.dot_general(
            query, key_ref[begin : begin + size, :], (((1,), (1,)), ((), ())), preferred_element_type=F32
        )
        term = dot(jnp.exp2(scores * scale).astype(BF16), value_ref[begin : begin + size, :])
        total = term if total is None else total + term
    return total


def early_kernel(keys, core_ref, allowed_ref, *refs):
    queries, contexts = refs[:3], refs[3 : 3 + len(keys)]
    query_ref, sums_ref, key_ref, value_ref = refs[3 + len(keys) :]
    first, second, third = queries
    rows = second.shape[0] // 2
    half = rows // 2
    query_ref[0:rows, :] = first[rows : 2 * rows, :]
    query_ref[rows : 2 * rows, :] = second[:rows, :]
    query_ref[2 * rows : 3 * rows, :] = third[:rows, :]
    query_ref[3 * rows : 4 * rows, :] = first[:rows, :]
    flip = core_ref[0] * half
    query_ref[pl.ds(pl.multiple_of(4 * rows + flip, 16), half), :] = third[2 * rows : 2 * rows + half, :]
    query_ref[pl.ds(pl.multiple_of(4 * rows + half - flip, 16), half), :] = third[2 * rows + half :, :]
    query_ref[5 * rows : 6 * rows, :] = first[2 * rows :, :]
    query_ref[6 * rows : 7 * rows, :] = second[rows:, :]
    query_ref[7 * rows :, :] = third[rows : 2 * rows, :]

    begin = 0
    for (place, back), context in zip(keys, contexts):
        span = slice(begin, begin + context.shape[0])
        allowed = allowed_ref[place : place + context.shape[0], back : back + 1]
        key_ref[span, :] = context[:, : key_ref.shape[1]]
        value_ref[span, :] = masked_values(context, allowed)
        begin += context.shape[0]

    def tile(index, _):
        part = pl.ds(pl.multiple_of(index * 256, 256), 256)
        sums_ref[part, :] = weighted_sums(query_ref[part, :], key_ref, value_ref, 4)
        return 0

    lax.fori_loop(0, query_ref.shape[0] // 256, tile, 0)


def late_kernel(
    place, allowed_ref, query_ref, sums_ref, one_ref, two_ref, same_ref, other_ref, *scratch
):
    key_ref, value_ref, attended_ref = scratch
    count, head_size = query_ref.shape
    rows = count // 8
    size = one_ref.shape[0]
    for back, context in ((1, one_ref), (2, two_ref)):
        span = slice((back - 1) * size, back * size)
        allowed = allowed_ref[place : place + size, back : back + 1]
        key_ref[span, :] = context[:, :head_size]
        value_ref[span, :] = masked_values(context, allowed)

    def tile(index, _):
        part = pl.ds(pl.multiple_of(index * 256, 256), 256)
        sums = sums_ref[part, :] + weighted_sums(query_ref[part, :], key_ref, value_ref, 1)
        attended_ref[part, :] = (sums[:, :head_size] / sums[:, head_size:]).astype(BF16)
        return 0

    lax.fori_loop(0, count // 256, tile, 0)
    other_ref[...] = attended_ref[: 5 * rows, :]
    same_ref[...] = attended_ref[3 * rows :, :]


def term_kernel(steps, core_ref, same_ref, far_ref, near_ref, opposite_ref, w_ref, w_other_ref, *outs):
    width = w_ref.shape[1] // 2
    rows = same_ref.shape[0] // 5
    for (step, side, _), out_ref in zip(steps, outs):
        start = (0 if step == 0 else 1 if step == STEPS else 1 + step) * rows
        begin = (start - 2 * rows) % (5 * rows)
        place = core_ref[0] if side == 0 else 1 - core_ref[0]
        columns = pl.ds(pl.multiple_of(place * width, 128), width)
        same = jnp.concatenate([same_ref[start : start + rows], far_ref[start : start + rows]], axis=1)
        other = jnp.concatenate(
            [near_ref[begin : begin + rows], opposite_ref[begin : begin + rows]], axis=1
        )
        term = dot(same, w_ref[:, columns]) + dot(other, w_other_ref[:, columns])
        out_ref[...] = term.astype(out_ref.dtype)


def vmem_call(kernel, out_shape, *operands, scalars=0, scratch=(), flops=1024):
    vmem = pl.BlockSpec(memory_space=pltpu.VMEM)
    return pl.pallas_call(
        kernel,
        out_shape=out_shape,
        in_specs=[pl.BlockSpec(memory_space=pltpu.SMEM)] * scalars + [vmem] * (len(operands) - scalars),
        out_specs=tuple([vmem] * len(out_shape)),
        scratch_shapes=scratch,
        compiler_params=pltpu.CompilerParams(vmem_limit_bytes=12 * 1024 * 1024),
        cost_estimate=pl.CostEstimate(flops=flops, bytes_accessed=1024, transcendentals=0),
        name="attend",
    )(*operands)


def on_device(latents, levels, window_mask, level_table, w_qkv, gain_q, gain_k, w_out):
    rows = latents.shape[1]
    width = latents.shape[2]
    model_width = w_qkv.shape[0]
    head_size = gain_q.shape[1]
    half = rows // 2
    mp_index = lax.axis_index("mp")
    space_index = lax.axis_index("space")
    core = lax.rem(mp_index, 2)
    chip = mp_index // 2

    own = latents[0]
    with jax.named_scope("own_rows_near"):
        near = swapped(own, 1)
    with jax.named_scope("own_rows_far"):
        far = swapped(own, 2)
    def in_core_order(mine, other):
        return jnp.concatenate([jnp.where(core == 0, mine, other), jnp.where(core == 0, other, mine)], axis=1)

    def ring(name, value):
        with jax.named_scope(name):
            return onward(value)

    def both(name, first, second):
        with jax.named_scope(name):
            return (first, second), (swapped(first, 1), swapped(second, 1))

    def core_half(block):
        return lax.dynamic_slice_in_dim(block, core * half, half, 0)

    a_0 = in_core_order(own, near)
    a_1 = ring("ring_a1", a_0)
    with jax.named_scope("own_rows_far_near"):
        far_near = swapped(after(far, a_1), 1)
    b_0 = in_core_order(far, far_near)
    b_1 = ring("ring_b1", b_0)

    level = after(levels, a_1)[0]
    own_mod = lax.dynamic_slice(level_table, (level, 0, 0), (1, 3, model_width))[0]
    gate = lax.dynamic_slice_in_dim(own_mod[2], mp_index * width, width, 0)
    gains = jnp.concatenate([gain_q, gain_k])
    mod_rows = jnp.stack([own_mod[0], 1.0 + own_mod[1]])

    w_own = w_qkv[:, 0, :]

    def projected(*pieces, carry=(), following=(), flops=1024):
        return project(chip, mod_rows, gains, w_own, pieces, carry, following, flops)

    def with_prior(name, context):
        with jax.named_scope(name):
            return context, shifted(context, 1), shifted(context, 2)

    a_2 = ring("ring_a2", a_1)
    b_2 = ring("ring_b2", b_1)
    a_3 = ring("ring_a3", a_2)
    query_01, context_01, done_01 = projected((a_0, b_0), *both("rows_1", a_1, b_1), following=(a_2,))
    contexts = [with_prior("prior_01", context_01)]
    b_3 = ring("ring_b3", after(b_2, done_01))
    a_4 = ring("ring_a4", core_half(a_3))
    b_4 = ring("ring_b4", core_half(b_3))
    def chip_columns(source, index):
        return lax.dynamic_slice_in_dim(source, index * 2 * width, 2 * width, 1)

    w_out_own = after(w_out[0], b_0)
    with jax.named_scope("out_weights_far"):
        out_far = swapped_chips(chip_columns(w_out_own, 1 - chip))
    out_rows = jnp.concatenate([chip_columns(w_out_own, chip), out_far])
    with jax.named_scope("out_weights_near"):
        out_other_rows = swapped(out_rows, 1)

    hop = [0] * rows + [sign * step for step in range(1, STEPS) for sign in (-1, 1) for _ in range(rows)]
    hop += [-STEPS] * half + [STEPS] * half
    within = list(range(rows)) * (2 * STEPS - 1) + list(range(half)) * 2
    first_half = [0] * (len(hop) - rows) + [1] * half + [-1] * half
    hop, within, first_half = (np.asarray(v, np.int32) for v in (hop, within, first_half))
    mask, here = after(window_mask[0], b_1), after(space_index, b_1)
    block = (here + hop * (1 - 2 * core) + SPACE) % SPACE
    extra = jnp.where(first_half == 0, 0, jnp.where(first_half > 0, core, 1 - core)) * half
    order = block * rows + within + extra
    pick = (order[:, None] == jnp.arange(rows * SPACE, dtype=jnp.int32)[None, :]).astype(BF16)
    allowed = lax.dot_general(
        pick, mask.astype(BF16), (((1,), (1,)), ((), ())), preferred_element_type=F32
    )

    query_2, context_2, done_2 = projected(*both("rows_2", a_2, b_2), following=(a_3, done_01, out_other_rows, allowed), flops=10**10)
    contexts.append(with_prior("prior_2", context_2))
    query_3, context_3, _ = projected(
        *both("rows_3", after(a_3, done_2), after(b_3, done_2)),
        *both("rows_4", a_4, b_4),
        following=(done_2,),
        flops=10**10,
    )
    contexts.append(with_prior("prior_3", context_3))

    keys, parts, begin = [], [], 0
    for context in contexts[:-1]:
        for back in range(3):
            keys.append((begin, back))
            parts.append(context[back])
        begin += context[0].shape[0]
    keys.append((begin, 0))
    parts.append(contexts[-1][0])
    count, last = rows * SPACE, contexts[-1][0].shape[0]
    early = sum(part.shape[0] for part in parts)

    def key_scratch(size):
        return [pltpu.VMEM((size, head_size), BF16), pltpu.VMEM((size, 2 * head_size), BF16)]

    query, sums = vmem_call(
        functools.partial(early_kernel, tuple(keys)),
        (
            jax.ShapeDtypeStruct((count, head_size), BF16),
            jax.ShapeDtypeStruct((count, 2 * head_size), F32),
        ),
        core.reshape(1),
        allowed,
        query_01,
        query_2,
        query_3,
        *parts,
        scalars=1,
        scratch=key_scratch(early),
        flops=10**10,
    )
    for_same, for_other = vmem_call(
        functools.partial(late_kernel, begin),
        (jax.ShapeDtypeStruct((5 * rows, head_size), BF16),) * 2,
        allowed,
        query,
        sums,
        *contexts[-1][1:],
        scratch=key_scratch(2 * last) + [pltpu.VMEM((count, head_size), BF16)],
    )
    with jax.named_scope("heads"):
        far_heads = swapped(for_same, 2)
        near_heads, opposite_heads = swapped(for_other, 1), swapped(for_other, 3)

    def terms(steps):
        return vmem_call(
            functools.partial(term_kernel, steps),
            tuple(jax.ShapeDtypeStruct((rows, width), BF16 if wide < 0 else F32) for _, _, wide in steps),
            core.reshape(1),
            for_same,
            far_heads,
            near_heads,
            opposite_heads,
            out_rows,
            out_other_rows,
            scalars=1,
        )

    first_b, first_a = terms(((STEPS - 1, 1, -1), (STEPS, 0, -1)))
    sum_b = ring("sum_b3", first_b)
    sum_a = ring("sum_a4", first_a)
    order = [(k, side) for k in range(STEPS - 1, 0, -1) for side in (0, 1) if (k, side) != (STEPS - 1, 1)]
    rest = dict(zip(order + [(0, 0)], terms(tuple((k, side, 1) for k, side in order + [(0, 0)]))))
    for k in range(STEPS - 1, 0, -1):
        if k > 1:
            sum_b = ring(f"sum_b{k - 1}", (rest[k - 1, 1] + sum_b.astype(F32)).astype(BF16))
        sum_a = ring(f"sum_a{k}", (rest[k, 0] + sum_a.astype(F32)).astype(BF16))
    branch_sum = rest[0, 0] + sum_a.astype(F32) + swapped(sum_b, 1).astype(F32)
    return (own.astype(F32) + gate * branch_sum).astype(BF16)[None]


def solution(mesh):
    in_specs = (
        P("frame", "space", "mp"),
        P("frame"),
        P("frame", None, None),
        P(),
        P(None, ("space", "mp"), None),
        P(("space", "mp"), None),
        P(("space", "mp"), None),
        P(("space", "mp"), None, None),
    )
    out_specs = P("frame", "space", "mp")
    return jax.shard_map(
        on_device, mesh=mesh, in_specs=in_specs, out_specs=out_specs, check_vma=False
    )
```
